768 devices in a mesh: dp: 96 (over z, x, core), table: 8 (over y).
Axes of the slice: x: 4, y: 8, z: 12, core: 2. Of those that a mesh axis runs over, the one named last changes fastest.
Arguments:
- hot_rows: bfloat16 [96, 8, 1024, 256], P('dp', 'table'), may hold values from -6 to 6
- hot_index: int32 [96, 8, 2048], P('dp', 'table'), may hold values from 0 to 1023
- hot_bag: int32 [96, 8, 2048], P('dp', 'table'), may hold values from 0 to 1023, never falling along the last dimension, each value on 1 to 4 neighbouring positions
- cold_rows: bfloat16 [96, 8, 1024, 128], P('dp', 'table'), may hold values from -6 to 6
- cold_index: int32 [96, 8, 2048], P('dp', 'table'), may hold values from 0 to 1023
- cold_bag: int32 [96, 8, 2048], P('dp', 'table'), may hold values from 0 to 1023, never falling along the last dimension, each value on 1 to 4 neighbouring positions
- hot_proj: bfloat16 [8, 256, 512], P('table'), may hold values from -0.375 to 0.375
- cold_proj: bfloat16 [8, 128, 512], P('table'), may hold values from -0.5 to 0.5
- cotangent: float32 [98304, 256], P(('dp', 'table')), may hold values from -6 to 6
Outputs:
- interaction: float32 [98304, 256], P(('dp', 'table'))
- grad_hot_proj: float32 [8, 256, 512], P('table')
- grad_cold_proj: float32 [8, 128, 512], P('table')
- grad_hot_rows: float32 [96, 8, 1024, 256], P('dp', 'table')
- grad_cold_rows: float32 [96, 8, 1024, 128], P('dp', 'table')
The draws below stay inside these ranges and needn't reach their ends.
Inputs may be any that keep to these rules, and one draw needn't show every extreme that they name: `hot_bag`: within each data group and table the bag numbers never fall; every sample of the group has a bag of 1 to 4 lookups. `cold_bag`: within each data group and table the bag numbers never fall; every sample of the group has a bag of 1 to 4 lookups.
All inputs are finite; a program needn't handle non-finite values.
Results may differ from the reference program's by a relative error of at most 0.0059.
Values may be sent and summed in bfloat16 or wider, within the bound.
A program may use at most 32 MiB of HBM per device.

```python
import math
import jax
import jax.numpy as jnp
import numpy as np
from jax import lax

WH = 256
WC = 128
DPROJ = 512
MAXPOOL = 4
B_DEV = 128
TOUCH_DEV = 1024
GB = 1024
LOOK = 2048
TABLES_H = 8
TABLES_C = 8
TABLES = 16
SAMPLES = 98304
N_DP = 96
N_TABLE = 8


def plant(entries, own_key, least, top_value):
    extent = entries.shape
    spot = [jax.random.randint(jax.random.fold_in(own_key, axis), (), 0, extent[axis]) for axis in range(len(extent))]
    entries = entries.at[tuple(spot)].set(least)
    longest = extent.index(max(extent))
    spot[longest] = (spot[longest] + 1) % extent[longest]
    return entries.at[tuple(spot)].set(top_value)


def block_levels(own_key, shape, cuts, smallest, high):
    gain = 1.0
    for dim, blocks in cuts:
        steps = jax.random.uniform(jax.random.fold_in(jax.random.fold_in(own_key, 6), dim), (blocks,), jnp.float32, smallest / len(cuts), high / len(cuts))
        gain = gain * jnp.repeat(jnp.exp(steps), shape[dim] // blocks).reshape((-1,) + (1,) * (len(shape) - 1 - dim))
    return gain


def rank_table(count, lean):
    portions = [(1 << 20) // math.isqrt(standing ** lean) + 1 for standing in range(1, count + 1)]
    deviation = 1 + sum(portions) // (1 << 30)
    return np.cumsum(np.array([max(1, weight // deviation) for weight in portions]))


def ranked(rng, dims, number_of, lean):
    table = rank_table(number_of, lean)
    pick = jax.random.randint(jax.random.fold_in(rng, 1), dims, 0, int(table[number_of - 1]))
    rank = jnp.searchsorted(jnp.asarray(table, jnp.int32), pick, side="right")
    return jax.random.permutation(jax.random.fold_in(rng, 2), number_of)[rank].astype(jnp.int32)


def length_profile(number_of, total, reach, slope):
    portions = [(1 << 20) // math.isqrt(standing ** slope) + 1 for standing in range(2, number_of + 1)]
    spare, counts = total - reach - (number_of - 1), [1] * (number_of - 1)
    while spare > 0:
        movable = [i for i in range(number_of - 1) if counts[i] < reach]
        pool, left = sum([portions[i] for i in movable]), spare
        for i in movable:
            extra = min(reach - counts[i], max(1, left * portions[i] // pool), spare)
            counts[i] = counts[i] + extra
            spare = spare - extra
    return np.array([reach] + counts)


def uneven(key, count, total, limit, lean):
    if count == 2:
        one = jax.random.randint(key, (), max(1, total - limit), min(limit, total - 1) + 1)
        return jnp.stack([one, total - one])
    tallies = jnp.asarray(length_profile(count, total, limit, lean), jnp.int32)
    pairs = (count - 1) // 2
    source_of, receiver = tallies[1:1 + 2 * pairs:2], tallies[2:2 + 2 * pairs:2]
    margin = jnp.minimum(source_of - 1, limit - receiver)
    passed = jax.random.randint(jax.random.fold_in(key, 1), (pairs,), 0, 1 << 20) % (margin + 1)
    tallies = tallies.at[1:1 + 2 * pairs:2].set(source_of - passed).at[2:2 + 2 * pairs:2].set(receiver + passed)
    return tallies[jax.random.permutation(jax.random.fold_in(key, 2), count)]


def gaussian(own_key, shape, spread, most, pieces=(), dtype=jnp.bfloat16):
    entries = spread * jax.random.normal(own_key, shape, jnp.float32)
    if pieces:
        entries = entries * block_levels(own_key, shape, pieces, -0.22, 0.18)
    return jnp.clip(entries, -most, most).astype(dtype)


def setup_inputs(seed: int = 0) -> dict:
    splits = jax.random.split(jax.random.key(seed), 10)
    return {
        "hot_rows": gaussian(splits[0], (N_DP, TABLES_H, TOUCH_DEV, WH), 1.0, 6.0, ((0, 96), (1, 8))),
        "hot_index": plant(ranked(splits[1], (N_DP, TABLES_H, LOOK), TOUCH_DEV, 2), jax.random.fold_in(splits[1], 3), 0, TOUCH_DEV - 1).astype(jnp.int32),
        "hot_bag": jax.vmap(lambda own: jnp.searchsorted(jnp.cumsum(uneven(own, GB, LOOK, MAXPOOL, 2)), jnp.arange(LOOK), side="right"))(jax.random.split(splits[2], N_DP * TABLES_H)).reshape((N_DP, TABLES_H, LOOK)).astype(jnp.int32),
        "cold_rows": gaussian(splits[3], (N_DP, TABLES_C, TOUCH_DEV, WC), 1.0, 6.0, ((0, 96), (1, 8))),
        "cold_index": plant(ranked(splits[4], (N_DP, TABLES_C, LOOK), TOUCH_DEV, 2), jax.random.fold_in(splits[4], 3), 0, TOUCH_DEV - 1).astype(jnp.int32),
        "cold_bag": jax.vmap(lambda own: jnp.searchsorted(jnp.cumsum(uneven(own, GB, LOOK, MAXPOOL, 2)), jnp.arange(LOOK), side="right"))(jax.random.split(splits[5], N_DP * TABLES_C)).reshape((N_DP, TABLES_C, LOOK)).astype(jnp.int32),
        "hot_proj": gaussian(splits[6], (TABLES_H, WH, DPROJ), WH ** -0.5, 0.375, ((0, 8),)),
        "cold_proj": gaussian(splits[7], (TABLES_C, WC, DPROJ), WC ** -0.5, 0.5, ((0, 8),)),
        "cotangent": gaussian(splits[8], (SAMPLES, TABLES * TABLES), 1.0, 6.0, ((0, 768),), jnp.float32),
    }


def pool_group(table_set, index_set, bag_set):

    def pool_table(table_rows, table_index, table_bag):
        picked = table_rows[table_index].astype(jnp.float32)
        return jax.ops.segment_sum(picked, table_bag, num_segments=B_DEV * N_TABLE, indices_are_sorted=True)
    return jax.vmap(pool_table)(table_set, index_set, bag_set).astype(jnp.bfloat16)

def project(pooled, weights):
    return jnp.einsum('tsw,twd->tsd', pooled.astype(jnp.float32), weights.astype(jnp.float32)).astype(jnp.bfloat16)

def spread_rows(back_grad, index_set, bag_set):

    def spread_table(table_grad, table_index, table_bag):
        picked = table_grad[table_bag].astype(jnp.float32)
        return jax.ops.segment_sum(picked, table_index, num_segments=TOUCH_DEV)
    return jax.vmap(spread_table)(back_grad, index_set, bag_set)

def reference(hot_rows, hot_index, hot_bag, cold_rows, cold_index, cold_bag, hot_proj, cold_proj, cotangent):
    groups = B_DEV * N_TABLE
    tables = TABLES_H + TABLES_C
    root_scale = 1.0 / math.sqrt(DPROJ)
    cot_groups = cotangent.reshape(N_DP, groups, tables, tables)

    def group_pass(running, inputs):
        h_rows, h_index, h_bag, c_rows, c_index, c_bag, cot_block = inputs
        hot_pooled = pool_group(h_rows, h_index, h_bag)
        cold_pooled = pool_group(c_rows, c_index, c_bag)
        features = jnp.concatenate([project(hot_pooled, hot_proj), project(cold_pooled, cold_proj)], axis=0)
        feat_wide = features.astype(jnp.float32)
        pair_dots = jnp.einsum('tsd,usd->stu', feat_wide, feat_wide) * root_scale
        symmetric = cot_block + jnp.transpose(cot_block, (0, 2, 1))
        grad_feat = (jnp.einsum('stu,usd->tsd', symmetric, feat_wide, precision=lax.Precision.HIGHEST) * root_scale).astype(jnp.bfloat16)
        grad_hot = grad_feat[:TABLES_H].astype(jnp.float32)
        grad_cold = grad_feat[TABLES_H:].astype(jnp.float32)
        hot_wgrad = jnp.einsum('tsw,tsd->twd', hot_pooled.astype(jnp.float32), grad_hot)
        cold_wgrad = jnp.einsum('tsw,tsd->twd', cold_pooled.astype(jnp.float32), grad_cold)
        hot_back = jnp.einsum('tsd,twd->tsw', grad_hot, hot_proj.astype(jnp.float32)).astype(jnp.bfloat16)
        cold_back = jnp.einsum('tsd,twd->tsw', grad_cold, cold_proj.astype(jnp.float32)).astype(jnp.bfloat16)
        hot_grads = spread_rows(hot_back, h_index, h_bag)
        cold_grads = spread_rows(cold_back, c_index, c_bag)
        updated = (running[0] + hot_wgrad, running[1] + cold_wgrad)
        return (updated, (pair_dots.reshape(groups, tables * tables), hot_grads, cold_grads))
    start = (jnp.zeros((TABLES_H, WH, DPROJ), jnp.float32), jnp.zeros((TABLES_C, WC, DPROJ), jnp.float32))
    totals, outputs = lax.scan(group_pass, start, (hot_rows, hot_index, hot_bag, cold_rows, cold_index, cold_bag, cot_groups))
    pair_all, hot_grads, cold_grads = outputs
    return (pair_all.reshape(N_DP * groups, tables * tables), totals[0] / N_DP, totals[1] / N_DP, hot_grads, cold_grads)
```

```python
import math

import jax
import jax.numpy as jnp
from jax import lax
from jax.experimental import pallas as pl
from jax.experimental.pallas import tpu as pltpu
from jax.sharding import PartitionSpec as P

F32 = jnp.float32
BF16 = jnp.bfloat16
MESH = pl.DeviceIdType.MESH
NY = 8
NX = 4
NZ = 12
WH, WC, D = 256, 128, 512
SB = 128
GB = 1024
LOOK = 2048
ROWS = 1024
BAND = 1152
VMEM_LIMIT = 48 * 1024 * 1024


def place():
    dp = lax.axis_index("dp")
    y = lax.axis_index("table")
    core = lax.rem(dp, 2)
    x = lax.rem(lax.div(dp, 2), NX)
    z = lax.div(dp, 2 * NX)
    return dp, y, z, x, core


def dot(a, b):
    return jnp.dot(a, b, preferred_element_type=F32)


def dot_nt(a, b):
    return lax.dot_general(a, b, (((1,), (1,)), ((), ())), preferred_element_type=F32)


def dot_tn(a, b):
    return lax.dot_general(a, b, (((0,), (0,)), ((), ())), preferred_element_type=F32)


def iota(shape, dim):
    return lax.broadcasted_iota(jnp.int32, shape, dim)


def split2(v):
    hi = v.astype(BF16)
    return hi, (v - hi.astype(F32)).astype(BF16)


def main_kernel(
    hot_rows, hot_index, hot_bag, cold_rows, cold_index, cold_bag, hot_proj, cold_proj, cot,
    inter, hot_grads, cold_grads, wpart,
    hot_picked, cold_picked, hot_send, cold_send, hot_recv, cold_recv,
    hot_w, cold_w, one_index, hot_at, cold_at, m_hi, m_lo, feat, grad,
    hot_bsend, cold_bsend, hot_back, cold_back,
    pool_sem, proj_sem, x_sem, core_sem, back_sem,
):
    dp, y, z, x, core = place()
    q = core * NX + x
    right = lax.rem(x + 1, NX)
    left = lax.rem(x + NX - 1, NX)
    far = lax.rem(x + 2, NX)

    def at_x(other):
        return ((z * NX + other) * 2 + core, y)

    sibling = (dp + 1 - 2 * core, y)

    barrier = pltpu.get_barrier_semaphore()
    for d in range(1, NY):
        pl.semaphore_signal(barrier, inc=1, device_id=(dp, lax.rem(y + d, NY)), device_id_type=MESH)
    for peer in (at_x(right), at_x(left), sibling):
        pl.semaphore_signal(barrier, inc=1, device_id=peer, device_id_type=MESH)
    pl.semaphore_wait(barrier, NY - 1 + 3)

    def hslice(block):
        return pl.ds(pl.multiple_of(block * 32, 32), 32)

    def cslice(block):
        return pl.ds(pl.multiple_of(block * 16, 16), 16)

    def proj_copies(d):
        peer = (dp, lax.rem(y + d, NY))
        return (
            pltpu.make_async_remote_copy(
                src_ref=hot_proj.at[0, hslice(q)], dst_ref=hot_w.at[y, hslice(q)],
                send_sem=proj_sem.at[0, d], recv_sem=proj_sem.at[1, d],
                device_id=peer, device_id_type=MESH),
            pltpu.make_async_remote_copy(
                src_ref=cold_proj.at[0, cslice(q)], dst_ref=cold_w.at[y, cslice(q)],
                send_sem=proj_sem.at[2, d], recv_sem=proj_sem.at[3, d],
                device_id=peer, device_id_type=MESH),
        )

    def start_proj(d, c):
        for copy in proj_copies(d):
            copy.start()
        return c

    lax.fori_loop(1, NY, start_proj, 0)
    hot_w[y, hslice(q)] = hot_proj[0, hslice(q)]
    cold_w[y, cslice(q)] = cold_proj[0, cslice(q)]

    lane = iota((128, 128), 1)

    def pick(index, rows, picked):
        def chunk(k, c):
            span = pl.ds(pl.multiple_of(k * 128, 128), 128)
            own = jnp.broadcast_to(index[0, :, span], (128, 128)).T
            hit = jnp.concatenate([(own == lane + 128 * r).astype(F32).astype(BF16) for r in range(8)], axis=1)
            picked[span, :] = dot(hit, rows[0, 0]).astype(BF16)
            return c

        lax.fori_loop(0, LOOK // 128, chunk, 0)

    def bag_hits(bag, block, samples, width):
        band = pl.ds(pl.multiple_of(block * SB, SB), width)
        ids = iota((samples, width), 0) + block * SB
        return band, (bag[0, :, band] == ids).astype(F32).astype(BF16)

    def pool_copy(which, d):
        send, recv = ((hot_send, hot_recv), (cold_send, cold_recv))[which]
        peer = lax.rem(y + d, NY)
        return pltpu.make_async_remote_copy(
            src_ref=send.at[peer], dst_ref=recv.at[y],
            send_sem=pool_sem.at[2 * which, d], recv_sem=pool_sem.at[2 * which + 1, d],
            device_id=(dp, peer), device_id_type=MESH)

    def pool(which, bag, picked):
        send, recv = ((hot_send, hot_recv), (cold_send, cold_recv))[which]

        def block(d, c):
            peer = lax.rem(y + d, NY)
            band, hits = bag_hits(bag, peer, SB, BAND)
            send[peer] = dot(hits, picked[band, :]).astype(BF16)
            pool_copy(which, d).start()
            return c

        lax.fori_loop(1, NY, block, 0)
        band, hits = bag_hits(bag, y, SB, BAND)
        recv[y] = dot(hits, picked[band, :]).astype(BF16)

    pick(hot_index, hot_rows, hot_picked)
    pool(0, hot_bag, hot_picked)
    pick(cold_index, cold_rows, cold_picked)
    pool(1, cold_bag, cold_picked)

    def x_copies(slot, tables, block, peer):
        return (
            pltpu.make_async_remote_copy(
                src_ref=hot_w.at[tables, hslice(block)], dst_ref=hot_w.at[tables, hslice(block)],
                send_sem=x_sem.at[0, slot], recv_sem=x_sem.at[1, slot],
                device_id=peer, device_id_type=MESH),
            pltpu.make_async_remote_copy(
                src_ref=cold_w.at[tables, cslice(block)], dst_ref=cold_w.at[tables, cslice(block)],
                send_sem=x_sem.at[2, slot], recv_sem=x_sem.at[3, slot],
                device_id=peer, device_id_type=MESH),
        )

    def core_copies(slot, block):
        return (
            pltpu.make_async_remote_copy(
                src_ref=hot_w.at[:, hslice(block)], dst_ref=hot_w.at[:, hslice(block)],
                send_sem=core_sem.at[0, slot], recv_sem=core_sem.at[1, slot],
                device_id=sibling, device_id_type=MESH),
            pltpu.make_async_remote_copy(
                src_ref=cold_w.at[:, cslice(block)], dst_ref=cold_w.at[:, cslice(block)],
                send_sem=core_sem.at[2, slot], recv_sem=core_sem.at[3, slot],
                device_id=sibling, device_id_type=MESH),
        )

    every, low, high = pl.ds(0, NY), pl.ds(0, NY // 2), pl.ds(NY // 2, NY // 2)
    steps_x = (
        x_copies(0, every, q, at_x(right)),
        x_copies(1, every, q, at_x(left)),
        x_copies(2, low, core * NX + left, at_x(right)),
        x_copies(3, high, core * NX + right, at_x(left)),
    )
    steps_core = tuple(core_copies(n, core * NX + other) for n, other in enumerate((x, left, right, far)))

    def start(copies):
        for copy in copies:
            copy.start()

    def arrived(copies):
        for copy in copies:
            copy.wait_recv()

    def proj_arrived(d, c):
        arrived(proj_copies(d))
        return c

    lax.fori_loop(1, NY, proj_arrived, 0)
    start(steps_x[0])
    start(steps_x[1])
    start(steps_core[0])

    def counts(index, bag, out):
        def onehot(k, c):
            rows = pl.ds(pl.multiple_of(k * 128, 128), 128)
            one_index[rows, :] = (index[0] == iota((128, LOOK), 0) + k * 128).astype(F32).astype(BF16)
            return c

        lax.fori_loop(0, ROWS // 128, onehot, 0)

        def column(j, c):
            width = BAND + SB
            first = jnp.minimum(2 * j, (LOOK - width) // SB)
            band = pl.ds(pl.multiple_of(first * SB, SB), width)
            ids = iota((2 * SB, width), 0) + 2 * SB * j
            hits = (bag[0, :, band] == ids).astype(F32).astype(BF16)
            out[:, pl.ds(pl.multiple_of(j * 2 * SB, 2 * SB), 2 * SB)] = dot_nt(one_index[:, band], hits).astype(BF16)
            return c

        lax.fori_loop(0, GB // (2 * SB), column, 0)

    row = iota((256, 256), 0)
    col = iota((256, 256), 1)
    row_hi, row_lo = lax.shift_right_logical(row, 4), lax.bitwise_and(row, 15)
    col_hi, col_lo = lax.shift_right_logical(col, 4), lax.bitwise_and(col, 15)

    def ones(mask):
        return mask.astype(F32).astype(BF16)

    turn = ones((row_hi == col_lo) & (row_lo == col_hi))
    widen = ones(row_lo == col_hi)
    narrow = ones(row_hi == col_lo)
    same_hi = row_hi == col_hi
    same_lo = row_lo == col_lo

    def spread_cot(g, c):
        rows = pl.ds(pl.multiple_of(g * 16, 16), 16)
        part = cot[rows, :]
        hi, lo = split2(part)
        sym = part + (dot(hi, turn) + dot(lo, turn))
        tall = jnp.where(same_hi, jnp.concatenate([sym] * 16, axis=0), 0.0)
        hi, lo = split2(tall)
        m_hi[g] = jnp.where(same_lo, dot(hi, widen), 0.0).astype(BF16)
        m_lo[g] = jnp.where(same_lo, dot(lo, widen), 0.0).astype(BF16)
        return c

    lax.fori_loop(0, SB // 16, spread_cot, 0)
    counts(hot_index, hot_bag, hot_at)

    arrived(steps_x[0])
    start(steps_x[2])
    start(steps_core[1])
    arrived(steps_x[1])
    start(steps_x[3])
    start(steps_core[2])

    counts(cold_index, cold_bag, cold_at)

    arrived(steps_x[2])
    arrived(steps_x[3])
    start(steps_core[3])
    for copies in steps_core:
        arrived(copies)

    def pool_arrived(d, c):
        pool_copy(0, d).wait_recv()
        pool_copy(1, d).wait_recv()
        return c

    lax.fori_loop(1, NY, pool_arrived, 0)

    def features(t, c):
        feat[t] = dot(hot_recv[t], hot_w[t]).astype(BF16)
        feat[NY + t] = dot(cold_recv[t], cold_w[t]).astype(BF16)
        return c

    lax.fori_loop(0, NY, features, 0)

    root_scale = 1.0 / math.sqrt(D)

    def sixteen(g, c):
        rows = pl.ds(pl.multiple_of(g * 16, 16), 16)
        block = feat[:, rows, :].reshape(256, D)
        gram = jnp.where(same_lo, dot_nt(block, block) * root_scale, 0.0)
        hi, lo = split2(gram)
        wide = jnp.where(same_hi, dot(hi, narrow) + dot(lo, narrow), 0.0)
        inter[rows, :] = jnp.sum(wide.reshape(16, 16, 256), axis=0)
        slope = (dot(m_hi[g], block) + dot(m_lo[g], block)) * root_scale
        grad[:, rows, :] = slope.astype(BF16).reshape(16, 16, D)
        return c

    lax.fori_loop(0, SB // 16, sixteen, 0)

    def back_copy(which, d):
        send, recv = ((hot_bsend, hot_back), (cold_bsend, cold_back))[which]
        peer = lax.rem(y + d, NY)
        return pltpu.make_async_remote_copy(
            src_ref=send.at[peer], dst_ref=recv.at[y],
            send_sem=back_sem.at[2 * which, d], recv_sem=back_sem.at[2 * which + 1, d],
            device_id=(dp, peer), device_id_type=MESH)

    def hot_return(d, c):
        peer = lax.rem(y + d, NY)
        hot_bsend[peer] = dot_nt(grad[peer], hot_w[peer]).astype(BF16)
        back_copy(0, d).start()
        return c

    def cold_return(d, c):
        peer = lax.rem(y + d, NY)
        cold_bsend[peer] = dot_nt(grad[NY + peer], cold_w[peer]).astype(BF16)
        back_copy(1, d).start()
        return c

    lax.fori_loop(1, NY, hot_return, 0)
    lax.fori_loop(1, NY, cold_return, 0)
    hot_back[y] = dot_nt(grad[y], hot_w[y]).astype(BF16)
    cold_back[y] = dot_nt(grad[NY + y], cold_w[y]).astype(BF16)

    def weight_part(t, c):
        wpart[:, t, 0:32, :] = dot_tn(hot_recv[t], grad[t]).astype(BF16).reshape(8, 32, D)
        wpart[:, t, 32:48, :] = dot_tn(cold_recv[t], grad[NY + t]).astype(BF16).reshape(8, 16, D)
        return c

    lax.fori_loop(0, NY, weight_part, 0)

    def back_arrived(which):
        def one(d, c):
            back_copy(which, d).wait_recv()
            return c

        lax.fori_loop(1, NY, one, 0)

    def spread(at, back, out, width):
        def rows_of(k, c):
            rows = pl.ds(pl.multiple_of(k * 256, 256), 256)
            out[0, 0, rows, :] = dot(at[rows, :], back[...].reshape(GB, width))
            return c

        lax.fori_loop(0, ROWS // 256, rows_of, 0)

    back_arrived(0)
    spread(hot_at, hot_back, hot_grads, WH)
    back_arrived(1)
    spread(cold_at, cold_back, cold_grads, WC)

    def sent(d, c):
        for copy in proj_copies(d):
            copy.wait_send()
        for which in range(2):
            pool_copy(which, d).wait_send()
            back_copy(which, d).wait_send()
        return c

    lax.fori_loop(1, NY, sent, 0)
    for copies in steps_x + steps_core:
        for copy in copies:
            copy.wait_send()


def reduce_kernel(
    wpart, hot_out, cold_out,
    core_recv, x_send, x_recv, z_send, z_recv, y_send, y_recv, comb,
    core_sem, x_sem, z_sem, y_sem, zg_sem, xg_sem, cg_sem,
):
    dp, y, z, x, core = place()
    q = core * NX + x
    sibling = (dp + 1 - 2 * core, y)

    def at_x(d):
        return ((z * NX + lax.rem(x + d, NX)) * 2 + core, y)

    def at_z(d):
        return ((lax.rem(z + d, NZ) * NX + x) * 2 + core, y)

    barrier = pltpu.get_barrier_semaphore()
    pl.semaphore_signal(barrier, inc=1, device_id=sibling, device_id_type=MESH)
    for d in range(1, NX):
        pl.semaphore_signal(barrier, inc=1, device_id=at_x(d), device_id_type=MESH)
    for d in range(1, NY):
        pl.semaphore_signal(barrier, inc=1, device_id=(dp, lax.rem(y + d, NY)), device_id_type=MESH)
    for d in range(1, NZ):
        pl.semaphore_signal(barrier, inc=1, device_id=at_z(d), device_id_type=MESH)
    pl.semaphore_wait(barrier, 1 + NX - 1 + NY - 1 + NZ - 1)

    def remote(src, dst, sems, slot, peer):
        return pltpu.make_async_remote_copy(
            src_ref=src, dst_ref=dst, send_sem=sems.at[0, slot], recv_sem=sems.at[1, slot],
            device_id=peer, device_id_type=MESH)


    def core_copy(k):
        return remote(wpart.at[(1 - core) * NX + k], core_recv.at[k], core_sem, k, sibling)

    def x_copy(d):
        return remote(x_send.at[lax.rem(x + d, NX)], x_recv.at[d], x_sem, d, at_x(d))

    def z_copy(d):
        return remote(z_send.at[lax.rem(z + d, NZ)], z_recv.at[d], z_sem, d, at_z(d))

    def y_copy(d):
        peer = lax.rem(y + d, NY)
        return remote(y_send.at[peer], y_recv.at[d], y_sem, d, (dp, peer))

    for d in range(1, NX + 1):
        core_copy(lax.rem(x + d, NX)).start()
    for d in range(1, NX):
        k = lax.rem(x + d, NX)
        core_copy(k).wait_recv()
        for t in range(NY):
            x_send[k, t] = (wpart[core * NX + k, t].astype(F32) + core_recv[k, t].astype(F32)).astype(BF16)
        x_copy(d).start()
    core_copy(x).wait_recv()

    for d in range(1, NX):
        x_copy(d).wait_recv()
    for t in range(NY):
        total = wpart[q, t].astype(F32) + core_recv[x, t].astype(F32)
        for d in range(1, NX):
            total = total + x_recv[d, t].astype(F32)
        total = total.astype(BF16)
        for rg in range(3):
            for cg in range(4):
                z_send[rg * 4 + cg, t] = total[16 * rg:16 * rg + 16, 128 * cg:128 * cg + 128]

    def z_start(d, c):
        z_copy(d).start()
        return c

    def z_wait(d, c):
        z_copy(d).wait_recv()
        return c

    lax.fori_loop(1, NZ, z_start, 0)
    lax.fori_loop(1, NZ, z_wait, 0)

    total = z_send[z].astype(F32)
    for d in range(1, NZ):
        total = total + z_recv[d].astype(F32)
    y_send[...] = total

    for d in range(1, NY):
        y_copy(d).start()
    final = y_send[y]
    for d in range(1, NY):
        y_copy(d).wait_recv()
        final = final + y_recv[d]
    final = final / (2 * NX * NZ)

    own = (
        pl.ds(pl.multiple_of(q * 48 + 16 * lax.div(z, 4), 16), 16),
        pl.ds(pl.multiple_of(128 * lax.rem(z, 4), 128), 128),
    )
    comb[own] = final

    def zg_copy(d):
        return remote(comb.at[own], comb.at[own], zg_sem, d, at_z(d))

    def xg_copy(d):
        rows = pl.ds(pl.multiple_of(q * 48, 16), 48)
        return remote(comb.at[rows], comb.at[rows], xg_sem, d, at_x(d))

    rows = pl.ds(pl.multiple_of(core * 192, 16), 192)
    cg_copy = remote(comb.at[rows], comb.at[rows], cg_sem, 0, sibling)

    def zg_start(d, c):
        zg_copy(d).start()
        return c

    def zg_wait(d, c):
        zg_copy(d).wait_recv()
        return c

    lax.fori_loop(1, NZ, zg_start, 0)
    lax.fori_loop(1, NZ, zg_wait, 0)
    for d in range(1, NX):
        xg_copy(d).start()
    for d in range(1, NX):
        xg_copy(d).wait_recv()
    cg_copy.start()
    cg_copy.wait_recv()

    for k in range(8):
        hot_out[0, 32 * k:32 * k + 32, :] = comb[48 * k:48 * k + 32, :]
        cold_out[0, 16 * k:16 * k + 16, :] = comb[48 * k + 32:48 * k + 48, :]

    cg_copy.wait_send()
    for k in range(NX):
        core_copy(k).wait_send()
    for d in range(1, NX):
        x_copy(d).wait_send()
        xg_copy(d).wait_send()
    for d in range(1, NY):
        y_copy(d).wait_send()

    def z_sent(d, c):
        z_copy(d).wait_send()
        zg_copy(d).wait_send()
        return c

    lax.fori_loop(1, NZ, z_sent, 0)


def vmem(*shape, dtype=BF16):
    return pltpu.VMEM(shape, dtype)


def local(
    hot_rows, hot_index, hot_bag, cold_rows, cold_index, cold_bag, hot_proj, cold_proj, cotangent
):
    whole = pl.BlockSpec(memory_space=pltpu.VMEM)
    sem = pltpu.SemaphoreType.DMA
    inter, hot_grads, cold_grads, wpart = pl.pallas_call(
        main_kernel,
        out_shape=(
            jax.ShapeDtypeStruct((SB, 256), F32),
            jax.ShapeDtypeStruct((1, 1, ROWS, WH), F32),
            jax.ShapeDtypeStruct((1, 1, ROWS, WC), F32),
            jax.ShapeDtypeStruct((8, NY, 48, D), BF16),
        ),
        in_specs=[whole] * 9,
        out_specs=(whole,) * 4,
        scratch_shapes=[
            vmem(LOOK, WH), vmem(LOOK, WC),
            vmem(NY, SB, WH), vmem(NY, SB, WC), vmem(NY, SB, WH), vmem(NY, SB, WC),
            vmem(NY, WH, D), vmem(NY, WC, D),
            vmem(ROWS, LOOK), vmem(ROWS, GB), vmem(ROWS, GB),
            vmem(8, 256, 256), vmem(8, 256, 256),
            vmem(2 * NY, SB, D), vmem(2 * NY, SB, D),
            vmem(NY, SB, WH), vmem(NY, SB, WC), vmem(NY, SB, WH), vmem(NY, SB, WC),
            sem((4, NY)), sem((4, NY)), sem((4, 4)), sem((4, 4)), sem((4, NY)),
        ],
        compiler_params=pltpu.CompilerParams(
            collective_id=0, has_side_effects=True, vmem_limit_bytes=VMEM_LIMIT),
    )(hot_rows, hot_index, hot_bag, cold_rows, cold_index, cold_bag, hot_proj, cold_proj, cotangent)
    hot_sum, cold_sum = pl.pallas_call(
        reduce_kernel,
        out_shape=(
            jax.ShapeDtypeStruct((1, WH, D), F32),
            jax.ShapeDtypeStruct((1, WC, D), F32),
        ),
        in_specs=[whole],
        out_specs=(whole,) * 2,
        scratch_shapes=[
            vmem(NX, NY, 48, D), vmem(NX, NY, 48, D), vmem(NX, NY, 48, D),
            vmem(NZ, NY, 16, 128), vmem(NZ, NY, 16, 128),
            vmem(NY, 16, 128, dtype=F32), vmem(NY, 16, 128, dtype=F32), vmem(384, D, dtype=F32),
            sem((2, NX)), sem((2, NX)), sem((2, NZ)), sem((2, NY)), sem((2, NZ)), sem((2, NX)), sem((2, 1)),
        ],
        compiler_params=pltpu.CompilerParams(
            collective_id=1, has_side_effects=True, vmem_limit_bytes=VMEM_LIMIT),
    )(wpart)
    return inter, hot_sum, cold_sum, hot_grads, cold_grads


def solution(mesh):
    return jax.shard_map(
        local,
        mesh=mesh,
        in_specs=(
            P("dp", "table", None, None),
            P("dp", "table", None),
            P("dp", "table", None),
            P("dp", "table", None, None),
            P("dp", "table", None),
            P("dp", "table", None),
            P("table", None, None),
            P("table", None, None),
            P(("dp", "table"), None),
        ),
        out_specs=(
            P(("dp", "table"), None),
            P("table", None, None),
            P("table", None, None),
            P("dp", "table", None, None),
            P("dp", "table", None, None),
        ),
        check_vma=False,
    )
```

```python
import math

import jax
import jax.numpy as jnp
from jax import lax
from jax.experimental import pallas as pl
from jax.experimental.pallas import tpu as pltpu
from jax.sharding import PartitionSpec as P

F32 = jnp.float32
BF16 = jnp.bfloat16
MESH = pl.DeviceIdType.MESH
NY = 8
NX = 4
NZ = 12
WH, WC, D = 256, 128, 512
SB = 128
GB = 1024
LOOK = 2048
ROWS = 1024
BAND = 1152
VMEM_LIMIT = 56 * 1024 * 1024
CHUNKS = 4
CW = D // CHUNKS
PICK = 512


def place():
    dp = lax.axis_index("dp")
    y = lax.axis_index("table")
    core = lax.rem(dp, 2)
    x = lax.rem(lax.div(dp, 2), NX)
    z = lax.div(dp, 2 * NX)
    return dp, y, z, x, core


def dot(a, b):
    return jnp.dot(a, b, preferred_element_type=F32)


def dot_nt(a, b):
    return lax.dot_general(a, b, (((1,), (1,)), ((), ())), preferred_element_type=F32)


def dot_tn(a, b):
    return lax.dot_general(a, b, (((0,), (0,)), ((), ())), preferred_element_type=F32)


def iota(shape, dim):
    return lax.broadcasted_iota(jnp.int32, shape, dim)


def split2(v):
    hi = v.astype(BF16)
    return hi, (v - hi.astype(F32)).astype(BF16)


def main_kernel(
    hot_rows_in, hot_index_in, hot_bag_in, cold_rows_in, cold_index_in, cold_bag_in, hot_proj_in, cold_proj_in, cot_in,
    inter, hot_sum, cold_sum, hot_grads, cold_grads,
    hot_rows, hot_index, hot_bag, cold_rows, cold_index, cold_bag, hot_proj, cold_proj, cot,
    hot_picked, cold_picked, hot_send, cold_send, hot_recv, cold_recv,
    hot_w, cold_w, one_index, hot_at, cold_at, m_hi, m_lo, feat, grad,
    hot_bsend, cold_bsend, hot_back, cold_back,
    wpart, core_recv, xs1, xr1, xs2, xr2, z_send, z_recv, y_send, y_recv, comb,
    in_sem, pool_sem, proj_sem, pair_sem, x_sem, core_sem, back_sem,
    wc_sem, wx1_sem, wx2_sem, wz_sem, wy_sem, zg_sem, xg_sem, cg_sem,
):
    dp, y, z, x, core = place()
    q = core * NX + x
    right = lax.rem(x + 1, NX)
    left = lax.rem(x + NX - 1, NX)
    far = lax.rem(x + 2, NX)

    loads = {}
    for n, (name, src, dst) in enumerate((
        ("hot_index", hot_index_in, hot_index), ("hot_rows", hot_rows_in, hot_rows), ("hot_bag", hot_bag_in, hot_bag),
        ("hot_proj", hot_proj_in, hot_proj), ("cold_proj", cold_proj_in, cold_proj),
        ("cold_index", cold_index_in, cold_index), ("cold_rows", cold_rows_in, cold_rows),
        ("cold_bag", cold_bag_in, cold_bag), ("cot", cot_in, cot),
    )):
        loads[name] = pltpu.make_async_copy(src, dst, in_sem.at[n])
        loads[name].start()

    def at_x(other):
        return ((z * NX + other) * 2 + core, y)

    def at_y(d):
        return (dp, lax.rem(y + d, NY))

    def at_z(d):
        return ((lax.rem(z + d, NZ) * NX + x) * 2 + core, y)

    sibling = (dp + 1 - 2 * core, y)

    def remote(src, dst, sems, slot, peer):
        return pltpu.make_async_remote_copy(
            src_ref=src, dst_ref=dst, send_sem=sems.at[(0,) + slot], recv_sem=sems.at[(1,) + slot],
            device_id=peer, device_id_type=MESH)

    barrier = pltpu.get_barrier_semaphore()

    def greet(peer):
        pl.semaphore_signal(barrier, inc=1, device_id=peer, device_id_type=MESH)

    def greet_y(d, c):
        greet(at_y(d))
        return c

    def greet_z(d, c):
        greet(at_z(d))
        return c

    lax.fori_loop(1, NY, greet_y, 0)
    for peer in (at_x(right), at_x(left), at_x(far), sibling):
        greet(peer)
    lax.fori_loop(1, NZ, greet_z, 0)

    def hslice(block):
        return pl.ds(pl.multiple_of(block * 32, 32), 32)

    def cslice(block):
        return pl.ds(pl.multiple_of(block * 16, 16), 16)

    pair = lax.rem(z, 2)

    def columns(n):
        block = lax.rem(2 * pair + n, CHUNKS)
        return pl.ds(pl.multiple_of(block * CW, CW), CW)

    def proj_copies(d, n):
        hot, cold = (hslice(q), columns(n)), (cslice(q), columns(n))
        return (
            remote(hot_proj.at[(0,) + hot], hot_w.at[(y,) + hot], proj_sem, (0, d, n), at_y(d)),
            remote(cold_proj.at[(0,) + cold], cold_w.at[(y,) + cold], proj_sem, (1, d, n), at_y(d)),
        )

    def pair_copies(n):
        hot, cold = hot_w.at[:, hslice(q), columns(n)], cold_w.at[:, cslice(q), columns(n)]
        return (
            remote(hot, hot, pair_sem, (0, n), at_z(1 - 2 * pair + NZ)),
            remote(cold, cold, pair_sem, (1, n), at_z(1 - 2 * pair + NZ)),
        )

    lane = iota((PICK, 128), 1)

    def pick(index, rows, picked):
        def chunk(k, c):
            own = jnp.concatenate([
                jnp.broadcast_to(index[0, :, pl.ds(pl.multiple_of(k * PICK + 128 * i, 128), 128)], (128, 128)).T
                for i in range(PICK // 128)
            ], axis=0)
            hit = jnp.concatenate([(own == lane + 128 * r).astype(F32).astype(BF16) for r in range(8)], axis=1)
            picked[pl.ds(pl.multiple_of(k * PICK, PICK), PICK), :] = dot(hit, rows[0, 0]).astype(BF16)
            return c

        lax.fori_loop(0, LOOK // PICK, chunk, 0, unroll=2)

    def bag_hits(bag, block, samples, width):
        band = pl.ds(pl.multiple_of(block * SB, SB), width)
        ids = iota((samples, width), 0) + block * SB
        return band, (bag[0, :, band] == ids).astype(F32).astype(BF16)

    def pool_copy(which, d):
        send, recv = ((hot_send, hot_recv), (cold_send, cold_recv))[which]
        peer = lax.rem(y + d, NY)
        return pltpu.make_async_remote_copy(
            src_ref=send.at[peer], dst_ref=recv.at[y],
            send_sem=pool_sem.at[2 * which, d], recv_sem=pool_sem.at[2 * which + 1, d],
            device_id=(dp, peer), device_id_type=MESH)

    def pool(which, bag, picked):
        send, recv = ((hot_send, hot_recv), (cold_send, cold_recv))[which]

        def block(d, c):
            peer = lax.rem(y + d, NY)
            band, hits = bag_hits(bag, peer, SB, BAND)
            send[peer] = dot(hits, picked[band, :]).astype(BF16)
            pool_copy(which, d).start()
            return c

        lax.fori_loop(1, NY, block, 0, unroll=True)
        band, hits = bag_hits(bag, y, SB, BAND)
        recv[y] = dot(hits, picked[band, :]).astype(BF16)

    loads["hot_index"].wait()
    loads["hot_rows"].wait()
    pick(hot_index, hot_rows, hot_picked)
    loads["hot_proj"].wait()
    loads["cold_proj"].wait()
    loads["hot_bag"].wait()
    pl.semaphore_wait(barrier, NY - 1 + NZ - 1 + 4)

    for n in range(2):
        def start_proj(d, c):
            for copy in proj_copies(d, n):
                copy.start()
            return c

        lax.fori_loop(1, NY, start_proj, 0)
    for n in range(2):
        hot_w[y, hslice(q), columns(n)] = hot_proj[0, hslice(q), columns(n)]
        cold_w[y, cslice(q), columns(n)] = cold_proj[0, cslice(q), columns(n)]

    def ways(tables, block, n, sems, slot, peer):
        hot = hot_w.at[tables, hslice(block), columns(n)]
        cold = cold_w.at[tables, cslice(block), columns(n)]
        return remote(hot, hot, sems, (0, slot, n), peer), remote(cold, cold, sems, (1, slot, n), peer)

    every, low, high = pl.ds(0, NY), pl.ds(0, NY // 2), pl.ds(NY // 2, NY // 2)
    steps_x = [(
        ways(every, q, n, x_sem, 0, at_x(right)),
        ways(every, q, n, x_sem, 1, at_x(left)),
        ways(low, core * NX + left, n, x_sem, 2, at_x(right)),
        ways(high, core * NX + right, n, x_sem, 3, at_x(left)),
    ) for n in range(CHUNKS)]
    steps_core = [tuple(
        ways(every, core * NX + other, n, core_sem, slot, sibling) for slot, other in enumerate((x, left, right, far))
    ) for n in range(CHUNKS)]

    def start(copies):
        for copy in copies:
            copy.start()

    def arrived(copies):
        for copy in copies:
            copy.wait_recv()

    def first_leg(n):
        def proj_arrived(d, c):
            arrived(proj_copies(d, n))
            return c

        lax.fori_loop(1, NY, proj_arrived, 0)
        start(steps_x[n][0])
        start(steps_x[n][1])
        start(pair_copies(n))
        start(steps_core[n][0])

    def second_leg(n):
        arrived(pair_copies(n))
        start(steps_x[2 + n][0])
        start(steps_x[2 + n][1])
        start(steps_core[2 + n][0])

    def third_leg(n):
        arrived(steps_x[n][0])
        start(steps_x[n][2])
        start(steps_core[n][1])
        arrived(steps_x[n][1])
        start(steps_x[n][3])
        start(steps_core[n][2])

    def fourth_leg(n):
        arrived(steps_x[n][2])
        arrived(steps_x[n][3])
        start(steps_core[n][3])

    pool(0, hot_bag, hot_picked)
    first_leg(0)
    loads["cold_index"].wait()
    loads["cold_rows"].wait()
    pick(cold_index, cold_rows, cold_picked)
    first_leg(1)
    loads["cold_bag"].wait()
    pool(1, cold_bag, cold_picked)
    second_leg(0)
    third_leg(0)
    second_leg(1)

    def onehots(index):
        def onehot(k, c):
            rows = pl.ds(pl.multiple_of(k * 128, 128), 128)
            one_index[rows, :] = (index[0] == iota((128, LOOK), 0) + k * 128).astype(F32).astype(BF16)
            return c

        lax.fori_loop(0, ROWS // 128, onehot, 0)

    def counts(bag, out, first, last):
        def column(j, c):
            width = BAND + SB
            band = pl.ds(pl.multiple_of(2 * j * SB, SB), width)
            ids = iota((2 * SB, width), 0) + 2 * SB * j
            hits = (bag[0, :, band] == ids).astype(F32).astype(BF16)
            out[:, pl.ds(pl.multiple_of(j * 2 * SB, 2 * SB), 2 * SB)] = dot_nt(one_index[:, band], hits).astype(BF16)
            return c

        lax.fori_loop(first, last, column, 0)

    row = iota((256, 256), 0)
    col = iota((256, 256), 1)
    row_hi, row_lo = lax.shift_right_logical(row, 4), lax.bitwise_and(row, 15)
    col_hi, col_lo = lax.shift_right_logical(col, 4), lax.bitwise_and(col, 15)

    def ones(mask):
        return mask.astype(F32).astype(BF16)

    turn = ones((row_hi == col_lo) & (row_lo == col_hi))
    widen = ones(row_lo == col_hi)
    narrow = ones(row_hi == col_lo)
    same_hi = row_hi == col_hi
    same_lo = row_lo == col_lo

    def spread_cot(g, c):
        rows = pl.ds(pl.multiple_of(g * 16, 16), 16)
        part = cot[rows, :]
        hi, lo = split2(part)
        sym = part + (dot(hi, turn) + dot(lo, turn))
        tall = jnp.where(same_hi, jnp.concatenate([sym] * 16, axis=0), 0.0)
        hi, lo = split2(tall)
        m_hi[g] = jnp.where(same_lo, dot(hi, widen), 0.0).astype(BF16)
        m_lo[g] = jnp.where(same_lo, dot(lo, widen), 0.0).astype(BF16)
        return c

    loads["cot"].wait()
    lax.fori_loop(0, SB // 16, spread_cot, 0, unroll=4)
    third_leg(1)
    onehots(hot_index)
    third_leg(2)
    counts(hot_bag, hot_at, 0, 2)
    third_leg(3)
    fourth_leg(0)
    fourth_leg(1)
    counts(hot_bag, hot_at, 2, 4)
    fourth_leg(2)
    fourth_leg(3)
    onehots(cold_index)
    for n in range(CHUNKS):
        for copies in steps_core[n]:
            arrived(copies)

    def hot_features(d, c):
        t = lax.rem(y - d + NY, NY)
        feat[t] = dot(hot_recv[t], hot_w[t]).astype(BF16)
        return c

    def cold_features(d, c):
        t = lax.rem(y - d + NY, NY)
        feat[NY + t] = dot(cold_recv[t], cold_w[t]).astype(BF16)
        return c

    def pool_arrived(which):
        def one(d, c):
            pool_copy(which, d).wait_recv()
            return c

        lax.fori_loop(1, NY, one, 0)

    pool_arrived(0)
    lax.fori_loop(0, NY, hot_features, 0, unroll=True)
    counts(cold_bag, cold_at, 0, 2)
    pool_arrived(1)
    lax.fori_loop(0, NY, cold_features, 0, unroll=True)

    root_scale = 1.0 / math.sqrt(D)

    def sixteen(g, c):
        rows = pl.ds(pl.multiple_of(g * 16, 16), 16)
        block = feat[:, rows, :].reshape(256, D)
        gram = jnp.where(same_lo, dot_nt(block, block) * root_scale, 0.0)
        hi, lo = split2(gram)
        wide = jnp.where(same_hi, dot(hi, narrow) + dot(lo, narrow), 0.0)
        inter[rows, :] = jnp.sum(wide.reshape(16, 16, 256), axis=0)
        slope = (dot(m_hi[g], block) + dot(m_lo[g], block)) * root_scale
        grad[:, rows, :] = slope.astype(BF16).reshape(16, 16, D)
        return c

    lax.fori_loop(0, SB // 16, sixteen, 0, unroll=4)


    def back_copy(which, d):
        send, recv = ((hot_bsend, hot_back), (cold_bsend, cold_back))[which]
        peer = lax.rem(y + d, NY)
        return pltpu.make_async_remote_copy(
            src_ref=send.at[peer], dst_ref=recv.at[y],
            send_sem=back_sem.at[2 * which, d], recv_sem=back_sem.at[2 * which + 1, d],
            device_id=(dp, peer), device_id_type=MESH)

    def hot_return(d, c):
        peer = lax.rem(y + d, NY)
        hot_bsend[peer] = dot_nt(grad[peer], hot_w[peer]).astype(BF16)
        back_copy(0, d).start()
        return c

    def cold_return(d, c):
        peer = lax.rem(y + d, NY)
        cold_bsend[peer] = dot_nt(grad[NY + peer], cold_w[peer]).astype(BF16)
        back_copy(1, d).start()
        return c

    def weight_part(t, c):
        wpart[:, t, 0:32, :] = dot_tn(hot_recv[t], grad[t]).astype(BF16).reshape(8, 32, D)
        wpart[:, t, 32:48, :] = dot_tn(cold_recv[t], grad[NY + t]).astype(BF16).reshape(8, 16, D)
        return c

    def wc_copy(k):
        pair = pl.ds(2 * k, 2)
        return remote(wpart.at[pl.ds((1 - core) * NX, NX), pair], core_recv.at[:, pair], wc_sem, (k,), sibling)

    def wx1_copy(k, way):
        return remote(xs1.at[k, way], xr1.at[k, way], wx1_sem, (k, way), at_x((right, left)[way]))

    def wx2_copy(k, way):
        return remote(xs2.at[k, way], xr2.at[k, way], wx2_sem, (k, way), at_x((right, left)[way]))

    def wz_copy(k, d):
        group = pl.ds(2 * k, 2)
        return remote(z_send.at[lax.rem(z + d, NZ), group], z_recv.at[d, group], wz_sem, (k, d), at_z(d))

    def wy_copy(d):
        return remote(y_send.at[lax.rem(y + d, NY)], y_recv.at[d], wy_sem, (d,), at_y(d))

    def both(other, t):
        return wpart[core * NX + other, t].astype(F32) + core_recv[other, t].astype(F32)

    def part(k):
        weight_part(2 * k, 0)
        weight_part(2 * k + 1, 0)
        wc_copy(k).start()

    def stage_core(k):
        wc_copy(k).wait_recv()
        xs1[k, 0, 0] = both(far, 2 * k).astype(BF16)
        xs1[k, 0, 1] = both(right, 2 * k + 1).astype(BF16)
        wx1_copy(k, 0).start()
        xs1[k, 1, 0] = both(far, 2 * k + 1).astype(BF16)
        xs1[k, 1, 1] = both(left, 2 * k).astype(BF16)
        wx1_copy(k, 1).start()

    def stage_x(k):
        wx1_copy(k, 0).wait_recv()
        xs2[k, 0] = (both(right, 2 * k) + xr1[k, 0, 0].astype(F32)).astype(BF16)
        wx2_copy(k, 0).start()
        wx1_copy(k, 1).wait_recv()
        xs2[k, 1] = (both(left, 2 * k + 1) + xr1[k, 1, 0].astype(F32)).astype(BF16)
        wx2_copy(k, 1).start()

    def stage_sum(k):
        wx2_copy(k, 0).wait_recv()
        wx2_copy(k, 1).wait_recv()
        for t, one, two in ((2 * k, xr2[k, 0], xr1[k, 1, 1]), (2 * k + 1, xr1[k, 0, 1], xr2[k, 1])):
            total = (both(x, t) + one.astype(F32) + two.astype(F32)).astype(BF16)
            for rg in range(3):
                for cg in range(4):
                    z_send[rg * 4 + cg, t] = total[16 * rg:16 * rg + 16, 128 * cg:128 * cg + 128]

    def stage_z(k):
        def one(d, c):
            wz_copy(k, d).start()
            return c

        lax.fori_loop(1, NZ, one, 0)

    def z_total(k):
        def one(d, c):
            wz_copy(k, d).wait_recv()
            return c

        lax.fori_loop(1, NZ, one, 0)
        group = slice(2 * k, 2 * k + 2)
        total = z_send[z, group].astype(F32)
        for d in range(1, NZ):
            total = total + z_recv[d, group].astype(F32)
        y_send[group] = total

    def back_arrived(which):
        def one(d, c):
            back_copy(which, d).wait_recv()
            return c

        lax.fori_loop(1, NY, one, 0)

    def spread(at, back, out, width):
        out[0, 0] = dot(at[...], back[...].reshape(GB, width))

    part(0)
    part(1)
    stage_core(0)
    part(2)
    stage_core(1)
    part(3)
    lax.fori_loop(1, NY, hot_return, 0, unroll=True)
    stage_core(2)
    stage_x(0)
    lax.fori_loop(1, NY, cold_return, 0, unroll=True)
    stage_core(3)
    stage_x(1)
    stage_sum(0)
    stage_z(0)
    stage_x(2)
    stage_sum(1)
    stage_z(1)
    hot_back[y] = dot_nt(grad[y], hot_w[y]).astype(BF16)
    cold_back[y] = dot_nt(grad[NY + y], cold_w[y]).astype(BF16)
    stage_x(3)
    stage_sum(2)
    stage_z(2)
    stage_sum(3)
    stage_z(3)
    counts(cold_bag, cold_at, 2, 4)
    z_total(0)
    z_total(1)
    z_total(2)
    z_total(3)
    for d in range(1, NY):
        wy_copy(d).start()
    back_arrived(0)
    spread(hot_at, hot_back, hot_grads, WH)
    final = y_send[y]
    for d in range(1, NY):
        wy_copy(d).wait_recv()
        final = final + y_recv[d]
    final = final / (2 * NX * NZ)

    own = (
        pl.ds(pl.multiple_of(q * 48 + 16 * lax.div(z, 4), 16), 16),
        pl.ds(pl.multiple_of(128 * lax.rem(z, 4), 128), 128),
    )
    comb[own] = final.astype(BF16)

    def zg_copy(d):
        return remote(comb.at[own], comb.at[own], zg_sem, (d,), at_z(d))

    def xg_copy(d):
        rows = pl.ds(pl.multiple_of(q * 48, 16), 48)
        return remote(comb.at[rows], comb.at[rows], xg_sem, (d,), at_x(lax.rem(x + d, NX)))

    rows = pl.ds(pl.multiple_of(core * 192, 16), 192)
    cg_copy = remote(comb.at[rows], comb.at[rows], cg_sem, (0,), sibling)

    def zg_start(d, c):
        zg_copy(d).start()
        return c

    def zg_wait(d, c):
        zg_copy(d).wait_recv()
        return c

    lax.fori_loop(1, NZ, zg_start, 0)
    back_arrived(1)
    spread(cold_at, cold_back, cold_grads, WC)
    lax.fori_loop(1, NZ, zg_wait, 0)
    for d in range(1, NX):
        xg_copy(d).start()
    for d in range(1, NX):
        xg_copy(d).wait_recv()
    cg_copy.start()
    cg_copy.wait_recv()

    for k in range(8):
        hot_sum[0, 32 * k:32 * k + 32, :] = comb[48 * k:48 * k + 32, :].astype(F32)
        cold_sum[0, 16 * k:16 * k + 16, :] = comb[48 * k + 32:48 * k + 48, :].astype(F32)

    def sent_y(d, c):
        for n in range(2):
            for copy in proj_copies(d, n):
                copy.wait_send()
        for which in range(2):
            pool_copy(which, d).wait_send()
            back_copy(which, d).wait_send()
        wy_copy(d).wait_send()
        return c

    def sent_z(d, c):
        for k in range(4):
            wz_copy(k, d).wait_send()
        zg_copy(d).wait_send()
        return c

    lax.fori_loop(1, NY, sent_y, 0)
    lax.fori_loop(1, NZ, sent_z, 0)
    for n in range(CHUNKS):
        for copies in steps_x[n] + steps_core[n]:
            for copy in copies:
                copy.wait_send()
    for n in range(2):
        for copy in pair_copies(n):
            copy.wait_send()
    for k in range(4):
        wc_copy(k).wait_send()
        for way in range(2):
            wx1_copy(k, way).wait_send()
            wx2_copy(k, way).wait_send()
    for d in range(1, NX):
        xg_copy(d).wait_send()
    cg_copy.wait_send()


def store_kernel(*refs):
    sources, targets, sems = refs[:5], refs[5:10], refs[10]
    copies = [pltpu.make_async_copy(sources[n], targets[n], sems.at[n]) for n in range(5)]
    for copy in copies:
        copy.start()
    for copy in copies:
        copy.wait()


def vmem(*shape, dtype=BF16):
    return pltpu.VMEM(shape, dtype)


def local(
    hot_rows, hot_index, hot_bag, cold_rows, cold_index, cold_bag, hot_proj, cold_proj, cotangent
):
    whole = pl.BlockSpec(memory_space=pltpu.VMEM)
    outside = pl.BlockSpec(memory_space=pl.ANY)
    sem = pltpu.SemaphoreType.DMA
    outs = (
        jax.ShapeDtypeStruct((SB, 256), F32),
        jax.ShapeDtypeStruct((1, WH, D), F32),
        jax.ShapeDtypeStruct((1, WC, D), F32),
        jax.ShapeDtypeStruct((1, 1, ROWS, WH), F32),
        jax.ShapeDtypeStruct((1, 1, ROWS, WC), F32),
    )
    ids = vmem(1, 1, LOOK, dtype=jnp.int32)
    args = (hot_rows, hot_index, hot_bag, cold_rows, cold_index, cold_bag, hot_proj, cold_proj, cotangent)
    results = pl.pallas_call(
        main_kernel,
        out_shape=outs,
        in_specs=[outside] * 9,
        out_specs=(whole,) * 5,
        scratch_shapes=[
            vmem(1, 1, ROWS, WH), ids, ids, vmem(1, 1, ROWS, WC), ids, ids,
            vmem(1, WH, D), vmem(1, WC, D), vmem(SB, 256, dtype=F32),
            vmem(LOOK, WH), vmem(LOOK, WC),
            vmem(NY, SB, WH), vmem(NY, SB, WC), vmem(NY, SB, WH), vmem(NY, SB, WC),
            vmem(NY, WH, D), vmem(NY, WC, D),
            vmem(ROWS, LOOK), vmem(ROWS, GB), vmem(ROWS, GB),
            vmem(8, 256, 256), vmem(8, 256, 256),
            vmem(2 * NY, SB, D), vmem(2 * NY, SB, D),
            vmem(NY, SB, WH), vmem(NY, SB, WC), vmem(NY, SB, WH), vmem(NY, SB, WC),
            vmem(8, NY, 48, D), vmem(NX, NY, 48, D),
            vmem(4, 2, 2, 48, D), vmem(4, 2, 2, 48, D), vmem(4, 2, 48, D), vmem(4, 2, 48, D),
            vmem(NZ, NY, 16, 128), vmem(NZ, NY, 16, 128),
            vmem(NY, 16, 128, dtype=F32), vmem(NY, 16, 128, dtype=F32), vmem(384, D),
            sem((9,)), sem((4, NY)), sem((2, 2, NY, 2)), sem((2, 2, 2)), sem((2, 2, 4, CHUNKS)), sem((2, 2, 4, CHUNKS)), sem((4, NY)),
            sem((2, 4)), sem((2, 4, 2)), sem((2, 4, 2)), sem((2, 4, NZ)), sem((2, NY)), sem((2, NZ)), sem((2, NX)), sem((2, 1)),
        ],
        compiler_params=pltpu.CompilerParams(
            collective_id=0, has_side_effects=True, vmem_limit_bytes=VMEM_LIMIT),
    )(*args)
    return tuple(pl.pallas_call(
        store_kernel,
        out_shape=outs,
        in_specs=[whole] * 5,
        out_specs=(outside,) * 5,
        scratch_shapes=[sem((5,))],
    )(*results))


def solution(mesh):
    return jax.shard_map(
        local,
        mesh=mesh,
        in_specs=(
            P("dp", "table", None, None),
            P("dp", "table", None),
            P("dp", "table", None),
            P("dp", "table", None, None),
            P("dp", "table", None),
            P("dp", "table", None),
            P("table", None, None),
            P("table", None, None),
            P(("dp", "table"), None),
        ),
        out_specs=(
            P(("dp", "table"), None),
            P("table", None, None),
            P("table", None, None),
            P("dp", "table", None, None),
            P("dp", "table", None, None),
        ),
        check_vma=False,
    )
```

```python
import math

import jax
import jax.numpy as jnp
from jax import lax
from jax.experimental import pallas as pl
from jax.experimental.pallas import tpu as pltpu
from jax.sharding import PartitionSpec as P

F32 = jnp.float32
BF16 = jnp.bfloat16
MESH = pl.DeviceIdType.MESH
NY = 8
NX = 4
NZ = 12
WH, WC, D = 256, 128, 512
SB = 128
GB = 1024
LOOK = 2048
ROWS = 1024
BAND = 1152
VMEM_LIMIT = 56 * 1024 * 1024
CHUNKS = 4
CW = D // CHUNKS
PICK = 512


def place():
    dp = lax.axis_index("dp")
    y = lax.axis_index("table")
    core = lax.rem(dp, 2)
    x = lax.rem(lax.div(dp, 2), NX)
    z = lax.div(dp, 2 * NX)
    return dp, y, z, x, core


def dot(a, b):
    return jnp.dot(a, b, preferred_element_type=F32)


def dot_nt(a, b):
    return lax.dot_general(a, b, (((1,), (1,)), ((), ())), preferred_element_type=F32)


def dot_tn(a, b):
    return lax.dot_general(a, b, (((0,), (0,)), ((), ())), preferred_element_type=F32)


def iota(shape, dim):
    return lax.broadcasted_iota(jnp.int32, shape, dim)


def split2(v):
    hi = v.astype(BF16)
    return hi, (v - hi.astype(F32)).astype(BF16)


def main_kernel(
    hot_rows_in, hot_index_in, hot_bag_in, cold_rows_in, cold_index_in, cold_bag_in, hot_proj_in, cold_proj_in, cot_in,
    inter, hot_sum, cold_sum, hot_grads, cold_grads,
    hot_rows, hot_index, hot_bag, cold_rows, cold_index, cold_bag, hot_proj, cold_proj, cot,
    hot_picked, cold_picked, hot_send, cold_send, hot_recv, cold_recv,
    proj_w, one_index, hot_at, cold_at, m_hi, m_lo, feat, grad,
    hot_bsend, cold_bsend, hot_back, cold_back,
    wpart, core_recv, xs1, xr1, xs2, xr2, z_send, z_recv, y_send, y_recv, comb,
    in_sem, pool_sem, proj_sem, pair_sem, x_sem, core_sem, back_sem,
    wc_sem, wx1_sem, wx2_sem, wz_sem, wy_sem, zg_sem, xg_sem, cg_sem,
):
    dp, y, z, x, core = place()
    q = core * NX + x
    right = lax.rem(x + 1, NX)
    left = lax.rem(x + NX - 1, NX)
    far = lax.rem(x + 2, NX)

    loads = {}
    for n, (name, src, dst) in enumerate((
        ("hot_index", hot_index_in, hot_index), ("hot_rows", hot_rows_in, hot_rows), ("hot_bag", hot_bag_in, hot_bag),
        ("hot_proj", hot_proj_in, hot_proj), ("cold_proj", cold_proj_in, cold_proj),
        ("cold_index", cold_index_in, cold_index), ("cold_rows", cold_rows_in, cold_rows),
        ("cold_bag", cold_bag_in, cold_bag), ("cot", cot_in, cot),
    )):
        loads[name] = pltpu.make_async_copy(src, dst, in_sem.at[n])
        loads[name].start()

    def at_x(other):
        return ((z * NX + other) * 2 + core, y)

    def at_y(d):
        return (dp, lax.rem(y + d, NY))

    def at_z(d):
        return ((lax.rem(z + d, NZ) * NX + x) * 2 + core, y)

    sibling = (dp + 1 - 2 * core, y)

    def remote(src, dst, sems, slot, peer):
        return pltpu.make_async_remote_copy(
            src_ref=src, dst_ref=dst, send_sem=sems.at[(0,) + slot], recv_sem=sems.at[(1,) + slot],
            device_id=peer, device_id_type=MESH)

    barrier = pltpu.get_barrier_semaphore()

    def greet(peer):
        pl.semaphore_signal(barrier, inc=1, device_id=peer, device_id_type=MESH)

    def greet_y(d, c):
        greet(at_y(d))
        return c

    def greet_z(d, c):
        greet(at_z(d))
        return c

    lax.fori_loop(1, NY, greet_y, 0)
    for peer in (at_x(right), at_x(left), at_x(far), sibling):
        greet(peer)
    lax.fori_loop(1, NZ, greet_z, 0)

    pair = lax.rem(z, 2)

    pair = lax.rem(z, 2)

    def columns(n):
        return lax.rem(2 * pair + n, CHUNKS)

    def proj_copy(d, n):
        mine = proj_w.at[columns(n), q, y]
        return remote(mine, mine, proj_sem, (d, n), at_y(d))

    def pair_copy(n):
        mine = proj_w.at[columns(n), q]
        return remote(mine, mine, pair_sem, (n,), at_z(1 - 2 * pair + NZ))

    def hot_weights(t):
        return jnp.concatenate([proj_w[n, :, t, 0:32, :].reshape(WH, CW) for n in range(CHUNKS)], axis=1)

    def cold_weights(t):
        return jnp.concatenate([proj_w[n, :, t, 32:48, :].reshape(WC, CW) for n in range(CHUNKS)], axis=1)

    lane = iota((PICK, 128), 1)

    def pick(index, rows, picked):
        def chunk(k, c):
            own = jnp.concatenate([
                jnp.broadcast_to(index[0, :, pl.ds(pl.multiple_of(k * PICK + 128 * i, 128), 128)], (128, 128)).T
                for i in range(PICK // 128)
            ], axis=0)
            hit = jnp.concatenate([(own == lane + 128 * r).astype(F32).astype(BF16) for r in range(8)], axis=1)
            picked[pl.ds(pl.multiple_of(k * PICK, PICK), PICK), :] = dot(hit, rows[0, 0]).astype(BF16)
            return c

        lax.fori_loop(0, LOOK // PICK, chunk, 0, unroll=2)

    def bag_hits(bag, block, samples, width):
        band = pl.ds(pl.multiple_of(block * SB, SB), width)
        ids = iota((samples, width), 0) + block * SB
        return band, (bag[0, :, band] == ids).astype(F32).astype(BF16)

    def pool_copy(which, d):
        send, recv = ((hot_send, hot_recv), (cold_send, cold_recv))[which]
        peer = lax.rem(y + d, NY)
        return pltpu.make_async_remote_copy(
            src_ref=send.at[peer], dst_ref=recv.at[y],
            send_sem=pool_sem.at[2 * which, d], recv_sem=pool_sem.at[2 * which + 1, d],
            device_id=(dp, peer), device_id_type=MESH)

    def pool(which, bag, picked):
        send, recv = ((hot_send, hot_recv), (cold_send, cold_recv))[which]

        def block(d, c):
            peer = lax.rem(y + d, NY)
            band, hits = bag_hits(bag, peer, SB, BAND)
            send[peer] = dot(hits, picked[band, :]).astype(BF16)
            pool_copy(which, d).start()
            return c

        lax.fori_loop(1, NY, block, 0, unroll=True)
        band, hits = bag_hits(bag, y, SB, BAND)
        recv[y] = dot(hits, picked[band, :]).astype(BF16)

    loads["hot_index"].wait()
    loads["hot_rows"].wait()
    pick(hot_index, hot_rows, hot_picked)
    loads["hot_proj"].wait()
    loads["cold_proj"].wait()
    loads["hot_bag"].wait()
    pl.semaphore_wait(barrier, NY - 1 + NZ - 1 + 4)

    for n in range(2):
        cols = pl.ds(pl.multiple_of(columns(n) * CW, CW), CW)
        proj_w[columns(n), q, y, 0:32, :] = hot_proj[0, pl.ds(pl.multiple_of(q * 32, 32), 32), cols]
        proj_w[columns(n), q, y, 32:48, :] = cold_proj[0, pl.ds(pl.multiple_of(q * 16, 16), 16), cols]

        def start_proj(d, c):
            proj_copy(d, n).start()
            return c

        lax.fori_loop(1, NY, start_proj, 0)

    def way(tables, block, n, sems, slot, peer):
        part = proj_w.at[columns(n), block, tables]
        return remote(part, part, sems, (slot, n), peer)

    every, low, high = pl.ds(0, NY), pl.ds(0, NY // 2), pl.ds(NY // 2, NY // 2)
    steps_x = [(
        way(every, q, n, x_sem, 0, at_x(right)),
        way(every, q, n, x_sem, 1, at_x(left)),
        way(low, core * NX + left, n, x_sem, 2, at_x(right)),
        way(high, core * NX + right, n, x_sem, 3, at_x(left)),
    ) for n in range(CHUNKS)]
    steps_core = [tuple(
        way(every, core * NX + other, n, core_sem, slot, sibling) for slot, other in enumerate((x, left, right, far))
    ) for n in range(CHUNKS)]

    def first_leg(n):
        def proj_arrived(d, c):
            proj_copy(d, n).wait_recv()
            return c

        lax.fori_loop(1, NY, proj_arrived, 0)
        steps_x[n][0].start()
        steps_x[n][1].start()
        pair_copy(n).start()
        steps_core[n][0].start()

    def second_leg(n):
        pair_copy(n).wait_recv()
        steps_x[2 + n][0].start()
        steps_x[2 + n][1].start()
        steps_core[2 + n][0].start()

    def third_leg(n):
        steps_x[n][0].wait_recv()
        steps_x[n][2].start()
        steps_core[n][1].start()
        steps_x[n][1].wait_recv()
        steps_x[n][3].start()
        steps_core[n][2].start()

    def fourth_leg(n):
        steps_x[n][2].wait_recv()
        steps_x[n][3].wait_recv()
        steps_core[n][3].start()

    pool(0, hot_bag, hot_picked)
    first_leg(0)
    loads["cold_index"].wait()
    loads["cold_rows"].wait()
    pick(cold_index, cold_rows, cold_picked)
    first_leg(1)
    loads["cold_bag"].wait()
    pool(1, cold_bag, cold_picked)
    second_leg(0)
    third_leg(0)
    second_leg(1)

    def onehots(index):
        def onehot(k, c):
            rows = pl.ds(pl.multiple_of(k * 128, 128), 128)
            one_index[rows, :] = (index[0] == iota((128, LOOK), 0) + k * 128).astype(F32).astype(BF16)
            return c

        lax.fori_loop(0, ROWS // 128, onehot, 0)

    def counts(bag, out, first, last):
        def column(j, c):
            width = BAND + SB
            band = pl.ds(pl.multiple_of(2 * j * SB, SB), width)
            ids = iota((2 * SB, width), 0) + 2 * SB * j
            hits = (bag[0, :, band] == ids).astype(F32).astype(BF16)
            out[:, pl.ds(pl.multiple_of(j * 2 * SB, 2 * SB), 2 * SB)] = dot_nt(one_index[:, band], hits).astype(BF16)
            return c

        lax.fori_loop(first, last, column, 0)

    row = iota((256, 256), 0)
    col = iota((256, 256), 1)
    row_hi, row_lo = lax.shift_right_logical(row, 4), lax.bitwise_and(row, 15)
    col_hi, col_lo = lax.shift_right_logical(col, 4), lax.bitwise_and(col, 15)

    def ones(mask):
        return mask.astype(F32).astype(BF16)

    turn = ones((row_hi == col_lo) & (row_lo == col_hi))
    widen = ones(row_lo == col_hi)
    narrow = ones(row_hi == col_lo)
    same_hi = row_hi == col_hi
    same_lo = row_lo == col_lo

    def spread_cot(g, c):
        rows = pl.ds(pl.multiple_of(g * 16, 16), 16)
        part = cot[rows, :]
        hi, lo = split2(part)
        sym = part + (dot(hi, turn) + dot(lo, turn))
        tall = jnp.where(same_hi, jnp.concatenate([sym] * 16, axis=0), 0.0)
        hi, lo = split2(tall)
        m_hi[g] = jnp.where(same_lo, dot(hi, widen), 0.0).astype(BF16)
        m_lo[g] = jnp.where(same_lo, dot(lo, widen), 0.0).astype(BF16)
        return c

    loads["cot"].wait()
    lax.fori_loop(0, SB // 16, spread_cot, 0, unroll=4)
    third_leg(1)
    onehots(hot_index)
    third_leg(2)
    counts(hot_bag, hot_at, 0, 2)
    third_leg(3)
    fourth_leg(0)
    fourth_leg(1)
    counts(hot_bag, hot_at, 2, 4)
    fourth_leg(2)
    fourth_leg(3)
    onehots(cold_index)
    for n in range(CHUNKS):
        for copy in steps_core[n]:
            copy.wait_recv()

    def hot_features(d, c):
        t = lax.rem(y - d + NY, NY)
        feat[t] = dot(hot_recv[t], hot_weights(t)).astype(BF16)
        return c

    def cold_features(d, c):
        t = lax.rem(y - d + NY, NY)
        feat[NY + t] = dot(cold_recv[t], cold_weights(t)).astype(BF16)
        return c

    def pool_arrived(which):
        def one(d, c):
            pool_copy(which, d).wait_recv()
            return c

        lax.fori_loop(1, NY, one, 0)

    pool_arrived(0)
    lax.fori_loop(0, NY, hot_features, 0, unroll=True)
    counts(cold_bag, cold_at, 0, 2)
    pool_arrived(1)
    lax.fori_loop(0, NY, cold_features, 0, unroll=True)

    root_scale = 1.0 / math.sqrt(D)

    def sixteen(g, c):
        rows = pl.ds(pl.multiple_of(g * 16, 16), 16)
        block = feat[:, rows, :].reshape(256, D)
        gram = jnp.where(same_lo, dot_nt(block, block) * root_scale, 0.0)
        hi, lo = split2(gram)
        wide = jnp.where(same_hi, dot(hi, narrow) + dot(lo, narrow), 0.0)
        inter[rows, :] = jnp.sum(wide.reshape(16, 16, 256), axis=0)
        slope = (dot(m_hi[g], block) + dot(m_lo[g], block)) * root_scale
        grad[:, rows, :] = slope.astype(BF16).reshape(16, 16, D)
        return c

    lax.fori_loop(0, SB // 16, sixteen, 0, unroll=4)


    def back_copy(which, d):
        send, recv = ((hot_bsend, hot_back), (cold_bsend, cold_back))[which]
        peer = lax.rem(y + d, NY)
        return pltpu.make_async_remote_copy(
            src_ref=send.at[peer], dst_ref=recv.at[y],
            send_sem=back_sem.at[2 * which, d], recv_sem=back_sem.at[2 * which + 1, d],
            device_id=(dp, peer), device_id_type=MESH)

    def hot_return(d, c):
        peer = lax.rem(y + d, NY)
        hot_bsend[peer] = dot_nt(grad[peer], hot_weights(peer)).astype(BF16)
        back_copy(0, d).start()
        return c

    def cold_return(d, c):
        peer = lax.rem(y + d, NY)
        cold_bsend[peer] = dot_nt(grad[NY + peer], cold_weights(peer)).astype(BF16)
        back_copy(1, d).start()
        return c

    def weight_part(t, c):
        wpart[:, t, 0:32, :] = dot_tn(hot_recv[t], grad[t]).astype(BF16).reshape(8, 32, D)
        wpart[:, t, 32:48, :] = dot_tn(cold_recv[t], grad[NY + t]).astype(BF16).reshape(8, 16, D)
        return c

    def wc_copy(k):
        pair = pl.ds(2 * k, 2)
        return remote(wpart.at[pl.ds((1 - core) * NX, NX), pair], core_recv.at[:, pair], wc_sem, (k,), sibling)

    def wx1_copy(k, way):
        return remote(xs1.at[k, way], xr1.at[k, way], wx1_sem, (k, way), at_x((right, left)[way]))

    def wx2_copy(k, way):
        return remote(xs2.at[k, way], xr2.at[k, way], wx2_sem, (k, way), at_x((right, left)[way]))

    def wz_copy(k, d):
        group = pl.ds(2 * k, 2)
        return remote(z_send.at[lax.rem(z + d, NZ), group], z_recv.at[d, group], wz_sem, (k, d), at_z(d))

    def wy_copy(d):
        return remote(y_send.at[lax.rem(y + d, NY)], y_recv.at[d], wy_sem, (d,), at_y(d))

    def both(other, t):
        return wpart[core * NX + other, t].astype(F32) + core_recv[other, t].astype(F32)

    def part(k):
        weight_part(2 * k, 0)
        weight_part(2 * k + 1, 0)
        wc_copy(k).start()

    def stage_core(k):
        wc_copy(k).wait_recv()
        xs1[k, 0, 0] = both(far, 2 * k).astype(BF16)
        xs1[k, 0, 1] = both(right, 2 * k + 1).astype(BF16)
        wx1_copy(k, 0).start()
        xs1[k, 1, 0] = both(far, 2 * k + 1).astype(BF16)
        xs1[k, 1, 1] = both(left, 2 * k).astype(BF16)
        wx1_copy(k, 1).start()

    def stage_x(k):
        wx1_copy(k, 0).wait_recv()
        xs2[k, 0] = (both(right, 2 * k) + xr1[k, 0, 0].astype(F32)).astype(BF16)
        wx2_copy(k, 0).start()
        wx1_copy(k, 1).wait_recv()
        xs2[k, 1] = (both(left, 2 * k + 1) + xr1[k, 1, 0].astype(F32)).astype(BF16)
        wx2_copy(k, 1).start()

    def stage_sum(k):
        wx2_copy(k, 0).wait_recv()
        wx2_copy(k, 1).wait_recv()
        for t, one, two in ((2 * k, xr2[k, 0], xr1[k, 1, 1]), (2 * k + 1, xr1[k, 0, 1], xr2[k, 1])):
            total = (both(x, t) + one.astype(F32) + two.astype(F32)).astype(BF16)
            for rg in range(3):
                for cg in range(4):
                    z_send[rg * 4 + cg, t] = total[16 * rg:16 * rg + 16, 128 * cg:128 * cg + 128]

    def stage_z(k):
        def one(d, c):
            wz_copy(k, d).start()
            return c

        lax.fori_loop(1, NZ, one, 0)

    def z_total(k):
        def one(d, c):
            wz_copy(k, d).wait_recv()
            return c

        lax.fori_loop(1, NZ, one, 0)
        group = slice(2 * k, 2 * k + 2)
        total = z_send[z, group].astype(F32)
        for d in range(1, NZ):
            total = total + z_recv[d, group].astype(F32)
        y_send[group] = total

    def back_arrived(which):
        def one(d, c):
            back_copy(which, d).wait_recv()
            return c

        lax.fori_loop(1, NY, one, 0)

    def spread(at, back, out, width):
        out[0, 0] = dot(at[...], back[...].reshape(GB, width))

    part(0)
    part(1)
    stage_core(0)
    part(2)
    stage_core(1)
    part(3)
    lax.fori_loop(1, NY, hot_return, 0, unroll=True)
    stage_core(2)
    stage_x(0)
    lax.fori_loop(1, NY, cold_return, 0, unroll=True)
    stage_core(3)
    stage_x(1)
    stage_sum(0)
    stage_z(0)
    stage_x(2)
    stage_sum(1)
    stage_z(1)
    hot_back[y] = dot_nt(grad[y], hot_weights(y)).astype(BF16)
    cold_back[y] = dot_nt(grad[NY + y], cold_weights(y)).astype(BF16)
    stage_x(3)
    stage_sum(2)
    stage_z(2)
    stage_sum(3)
    stage_z(3)
    counts(cold_bag, cold_at, 2, 4)

    def sent_forward(d, c):
        for n in range(2):
            proj_copy(d, n).wait_send()
            pool_copy(n, d).wait_send()
        return c

    lax.fori_loop(1, NY, sent_forward, 0)
    for n in range(CHUNKS):
        for copy in steps_x[n] + steps_core[n]:
            copy.wait_send()
    for n in range(2):
        pair_copy(n).wait_send()
    for k in range(4):
        wc_copy(k).wait_send()
        for way in range(2):
            wx1_copy(k, way).wait_send()
            wx2_copy(k, way).wait_send()

    z_total(0)
    z_total(1)
    z_total(2)
    z_total(3)
    for d in range(1, NY):
        wy_copy(d).start()
    back_arrived(0)
    spread(hot_at, hot_back, hot_grads, WH)
    final = y_send[y]
    for d in range(1, NY):
        wy_copy(d).wait_recv()
        final = final + y_recv[d]
    final = final / (2 * NX * NZ)

    own = comb.at[q, z]
    own[...] = final.astype(BF16)

    def zg_copy(d):
        return remote(own, own, zg_sem, (d,), at_z(d))

    def xg_copy(d):
        return remote(comb.at[q], comb.at[q], xg_sem, (d,), at_x(lax.rem(x + d, NX)))

    rows = pl.ds(core * NX, NX)
    cg_copy = remote(comb.at[rows], comb.at[rows], cg_sem, (0,), sibling)

    def zg_start(d, c):
        zg_copy(d).start()
        return c

    def zg_wait(d, c):
        zg_copy(d).wait_recv()
        return c

    lax.fori_loop(1, NZ, zg_start, 0)
    back_arrived(1)
    spread(cold_at, cold_back, cold_grads, WC)

    def sent_y(d, c):
        back_copy(0, d).wait_send()
        back_copy(1, d).wait_send()
        wy_copy(d).wait_send()
        return c

    def sent_z(d, c):
        for k in range(4):
            wz_copy(k, d).wait_send()
        return c

    def sent_zg(d, c):
        zg_copy(d).wait_send()
        return c

    lax.fori_loop(1, NY, sent_y, 0)
    lax.fori_loop(1, NZ, sent_z, 0)
    lax.fori_loop(1, NZ, zg_wait, 0)
    for d in range(1, NX):
        xg_copy(d).start()
    lax.fori_loop(1, NZ, sent_zg, 0)
    for d in range(1, NX):
        xg_copy(d).wait_recv()
    cg_copy.start()
    cg_copy.wait_recv()

    for k in range(8):
        for cg in range(4):
            cols = slice(128 * cg, 128 * cg + 128)
            hot_sum[0, 32 * k:32 * k + 16, cols] = comb[k, cg].astype(F32)
            hot_sum[0, 32 * k + 16:32 * k + 32, cols] = comb[k, 4 + cg].astype(F32)
            cold_sum[0, 16 * k:16 * k + 16, cols] = comb[k, 8 + cg].astype(F32)

    for d in range(1, NX):
        xg_copy(d).wait_send()
    cg_copy.wait_send()


def store_kernel(*refs):
    sources, targets, sems = refs[:5], refs[5:10], refs[10]
    copies = [pltpu.make_async_copy(sources[n], targets[n], sems.at[n]) for n in range(5)]
    for copy in copies:
        copy.start()
    for copy in copies:
        copy.wait()


def vmem(*shape, dtype=BF16):
    return pltpu.VMEM(shape, dtype)


def local(
    hot_rows, hot_index, hot_bag, cold_rows, cold_index, cold_bag, hot_proj, cold_proj, cotangent
):
    whole = pl.BlockSpec(memory_space=pltpu.VMEM)
    outside = pl.BlockSpec(memory_space=pl.ANY)
    sem = pltpu.SemaphoreType.DMA
    outs = (
        jax.ShapeDtypeStruct((SB, 256), F32),
        jax.ShapeDtypeStruct((1, WH, D), F32),
        jax.ShapeDtypeStruct((1, WC, D), F32),
        jax.ShapeDtypeStruct((1, 1, ROWS, WH), F32),
        jax.ShapeDtypeStruct((1, 1, ROWS, WC), F32),
    )
    ids = vmem(1, 1, LOOK, dtype=jnp.int32)
    args = (hot_rows, hot_index, hot_bag, cold_rows, cold_index, cold_bag, hot_proj, cold_proj, cotangent)
    results = pl.pallas_call(
        main_kernel,
        out_shape=outs,
        in_specs=[outside] * 9,
        out_specs=(whole,) * 5,
        scratch_shapes=[
            vmem(1, 1, ROWS, WH), ids, ids, vmem(1, 1, ROWS, WC), ids, ids,
            vmem(1, WH, D), vmem(1, WC, D), vmem(SB, 256, dtype=F32),
            vmem(LOOK, WH), vmem(LOOK, WC),
            vmem(NY, SB, WH), vmem(NY, SB, WC), vmem(NY, SB, WH), vmem(NY, SB, WC),
            vmem(CHUNKS, 8, NY, 48, CW),
            vmem(ROWS, LOOK), vmem(ROWS, GB), vmem(ROWS, GB),
            vmem(8, 256, 256), vmem(8, 256, 256),
            vmem(2 * NY, SB, D), vmem(2 * NY, SB, D),
            vmem(NY, SB, WH), vmem(NY, SB, WC), vmem(NY, SB, WH), vmem(NY, SB, WC),
            vmem(8, NY, 48, D), vmem(NX, NY, 48, D),
            vmem(4, 2, 2, 48, D), vmem(4, 2, 2, 48, D), vmem(4, 2, 48, D), vmem(4, 2, 48, D),
            vmem(NZ, NY, 16, 128), vmem(NZ, NY, 16, 128),
            vmem(NY, 16, 128, dtype=F32), vmem(NY, 16, 128, dtype=F32), vmem(8, NZ, 16, 128),
            sem((9,)), sem((4, NY)), sem((2, NY, 2)), sem((2, 2)), sem((2, 4, CHUNKS)), sem((2, 4, CHUNKS)), sem((4, NY)),
            sem((2, 4)), sem((2, 4, 2)), sem((2, 4, 2)), sem((2, 4, NZ)), sem((2, NY)), sem((2, NZ)), sem((2, NX)), sem((2, 1)),
        ],
        compiler_params=pltpu.CompilerParams(
            collective_id=0, has_side_effects=True, vmem_limit_bytes=VMEM_LIMIT),
    )(*args)
    return tuple(pl.pallas_call(
        store_kernel,
        out_shape=outs,
        in_specs=[whole] * 5,
        out_specs=(outside,) * 5,
        scratch_shapes=[sem((5,))],
    )(*results))


def solution(mesh):
    return jax.shard_map(
        local,
        mesh=mesh,
        in_specs=(
            P("dp", "table", None, None),
            P("dp", "table", None),
            P("dp", "table", None),
            P("dp", "table", None, None),
            P("dp", "table", None),
            P("dp", "table", None),
            P("table", None, None),
            P("table", None, None),
            P(("dp", "table"), None),
        ),
        out_specs=(
            P(("dp", "table"), None),
            P("table", None, None),
            P("table", None, None),
            P("dp", "table", None, None),
            P("dp", "table", None, None),
        ),
        check_vma=False,
    )
```
